512 devices in a mesh: blk: 512 (over x, y, z, core).
Axes of the slice: x: 4, y: 8, z: 8, core: 2. Of those that a mesh axis runs over, the one named last changes fastest.
Arguments:
- images: float32 [131072, 768], P('blk'), may hold values from -6 to 6
- texts: float32 [131072, 768], P('blk'), may hold values from -6 to 6
Outputs:
- pair_loss: float32 [131072], P('blk')
- image_grad: float32 [131072, 768], P('blk')
- text_grad: float32 [131072, 768], P('blk')
The draws below stay inside these ranges and needn't reach their ends.
All inputs are finite; a program needn't handle non-finite values.
Results may differ from the reference program's by a relative error of at most 0.0003.
Values sent between devices are 32-bit elements; how exact they have to be, the bound alone decides.
No kernel may reach another device: no remote copies, remote signals or barrier semaphores. Data moves between devices by JAX's collectives and lax.ppermute only.
A program may use at most 64 MiB of HBM per device.

```python
import math
import jax
import jax.numpy as jnp
from jax import lax

EMBED_WIDTH = 768
PAIRS_DEV = 256
CYCLE = 3
PAIRS = 131072
WINDOW = 1792
N_BLK = 512


def shard_levels(stream_key, dims, split, least, largest):
    loudness = 1.0
    for dim, parts in split:
        draws = jax.random.uniform(jax.random.fold_in(jax.random.fold_in(stream_key, 6), dim), (parts,), jnp.float32, least / len(split), largest / len(split))
        loudness = loudness * jnp.repeat(jnp.exp(draws), dims[dim] // parts).reshape((-1,) + (1,) * (len(dims) - 1 - dim))
    return loudness


def normal_values(rng, shape, width, most, pieces=(), kind=jnp.bfloat16):
    loudness = shard_levels(rng, shape, pieces, -0.22, 0.18) if pieces else 1.0
    values = jax.random.normal(rng, shape, jnp.float32) * width * loudness
    return jnp.minimum(jnp.maximum(values, -most), most).astype(kind)


def setup_inputs(seed: int = 0) -> dict:
    arg_keys = jax.random.split(jax.random.key(seed), 3)
    return {
        "images": normal_values(arg_keys[0], (PAIRS, EMBED_WIDTH), 1.0, 6.0, ((0, 512),), jnp.float32),
        "texts": normal_values(arg_keys[1], (PAIRS, EMBED_WIDTH), 1.0, 6.0, ((0, 512),), jnp.float32),
    }


softness_factor = 2.0
logit_bias = -4.0

def window_terms(own, others):
    logit_scale = softness_factor / math.sqrt(EMBED_WIDTH)
    dots = jnp.einsum('id,wjd->wij', own, others, precision=lax.Precision.HIGHEST)
    logits = logit_scale * dots + logit_bias
    rows = jnp.arange(PAIRS_DEV)
    diagonal = rows[:, None] == rows[None, :]
    centre = (jnp.arange(2 * CYCLE + 1) == CYCLE)[:, None, None]
    labels = jnp.where(centre & diagonal[None, :, :], 1.0, -1.0).astype(jnp.float32)
    signed = labels * logits
    losses = -lax.optimization_barrier(jnp.sum(jax.nn.log_sigmoid(signed), axis=(0, 2))) / WINDOW
    coefs = -labels * jax.nn.sigmoid(-signed)
    grads = jnp.einsum('wij,wjd->id', coefs, others, precision=lax.Precision.HIGHEST) * logit_scale
    return (losses, grads)

def reference(images, texts):
    image_blocks = images.reshape(N_BLK, PAIRS_DEV, EMBED_WIDTH)
    caption_blocks = texts.reshape(N_BLK, PAIRS_DEV, EMBED_WIDTH)
    offsets = jnp.arange(-CYCLE, CYCLE + 1).astype(jnp.int32)

    def image_side(centre):
        index = ((centre + offsets) % N_BLK).astype(jnp.int32)
        return window_terms(image_blocks[centre], jnp.take(caption_blocks, index, axis=0))

    def text_side(centre):
        index = ((centre + offsets) % N_BLK).astype(jnp.int32)
        return window_terms(caption_blocks[centre], jnp.take(image_blocks, index, axis=0))[1]
    centres = jnp.arange(N_BLK).astype(jnp.int32)
    losses, image_grad = lax.map(image_side, centres)
    text_grad = lax.map(text_side, centres)
    return (losses.reshape(PAIRS), image_grad.reshape(PAIRS, EMBED_WIDTH), text_grad.reshape(PAIRS, EMBED_WIDTH))
```

```python
import functools
import math

import jax
import jax.numpy as jnp
from jax import lax
from jax.experimental import pallas as pl
from jax.experimental.pallas import tpu as pltpu
from jax.sharding import PartitionSpec as P

CYCLE = 3
softness_factor = 2.0
logit_bias = -4.0
EXTRA = 8
VMEM_LIMIT = 24 * 1024 * 1024


def permuted(value, target):
    count = lax.axis_size("blk")
    return lax.ppermute(value, "blk", [(i, target(i) % count) for i in range(count)])


def sibling(value):
    return permuted(value, lambda i: i ^ 1)


def outward(value):
    return permuted(value, lambda i: i - 2 if i % 2 else i + 2)


def inward(value):
    return permuted(value, lambda i: i + 2 if i % 2 else i - 2)


def across(value):
    return permuted(value, lambda i: i + 1 if i % 2 else i - 1)


def halves(x):
    high = x.astype(jnp.bfloat16)
    return high, (x - high.astype(jnp.float32)).astype(jnp.bfloat16)


def product(a, b, contract_b):
    dims = (((1,), (contract_b,)), ((), ()))
    dot = functools.partial(lax.dot_general, dimension_numbers=dims, preferred_element_type=jnp.float32)
    return dot(a[0], b[0]) + (dot(a[0], b[1]) + dot(a[1], b[0]))


def terms(own, block, positive=False, loss=False):
    scale = softness_factor / math.sqrt(own[0].shape[1])
    x = scale * product(own, block, 1) + logit_bias
    if positive:
        shape = x.shape
        diagonal = lax.broadcasted_iota(jnp.int32, shape, 0) == lax.broadcasted_iota(jnp.int32, shape, 1)
        x = jnp.where(diagonal, -x, x)
    e = jnp.exp(-jnp.abs(x))
    r = 1.0 / (1.0 + e)
    coefs = jnp.where(x >= 0, r, e * r)
    if positive:
        coefs = jnp.where(diagonal, -coefs, coefs)
    if not loss:
        return coefs, None
    series = e * (1.0 - e * (0.5 - e * (1.0 / 3.0 - e * (0.25 - e * 0.2))))
    each = jnp.maximum(x, 0.0) + jnp.where(e < 0.0625, series, jnp.log(1.0 + e))
    return coefs, each[:, :128] + each[:, 128:]


def as_row(loss):
    return jnp.sum(loss.T, axis=0, keepdims=True)


def first_kernel(loss, own_ref, own_sib_ref, partner_ref, partner_sib_ref, block_ref, mine_ref, theirs_ref):
    rows = own_ref.shape[0]
    own, own_sib = halves(own_ref[...]), halves(own_sib_ref[...])
    total, lost = 0.0, 0.0
    for ref, positive in ((partner_ref, True), (partner_sib_ref, False), (block_ref, False)):
        block = halves(ref[...])
        coefs, each = terms(own, block, positive, loss)
        total = total + product(halves(coefs), block, 0)
        if loss:
            lost = lost + each
    mine_ref[:rows, :] = total
    coefs, each = terms(own_sib, block, False, loss)
    theirs_ref[:rows, :] = product(halves(coefs), block, 0)
    if loss:
        mine_ref[rows : rows + 1, : rows] = as_row(lost)
        theirs_ref[rows : rows + 1, : rows] = as_row(each)


def second_kernel(loss, own_ref, own_sib_ref, block_ref, mine_in, theirs_in, mine_ref, theirs_ref):
    rows = own_ref.shape[0]
    block = halves(block_ref[...])
    for ref, given, out in ((own_sib_ref, theirs_in, theirs_ref), (own_ref, mine_in, mine_ref)):
        coefs, each = terms(halves(ref[...]), block, False, loss)
        out[:rows, :] = given[:rows, :] + product(halves(coefs), block, 0)
        if loss:
            out[rows : rows + 1, : rows] = given[rows : rows + 1, : rows] + as_row(each)


def last_kernel(loss, own_ref, block_ref, mine_in, from_sib, grad_ref, *loss_ref):
    rows, width = own_ref.shape
    scale = softness_factor / math.sqrt(width)
    block = halves(block_ref[...])
    coefs, each = terms(halves(own_ref[...]), block, False, loss)
    grad_ref[...] = scale * (mine_in[:rows, :] + from_sib[:rows, :] + product(halves(coefs), block, 0))
    if loss:
        total = mine_in[rows : rows + 1, : rows] + from_sib[rows : rows + 1, : rows] + as_row(each)
        loss_ref[0][...] = total * (1.0 / ((2 * CYCLE + 1) * rows))


def call(kernel, loss, outs, *args):
    return pl.pallas_call(
        functools.partial(kernel, loss),
        out_shape=[jax.ShapeDtypeStruct(s, jnp.float32) for s in outs],
        compiler_params=pltpu.CompilerParams(vmem_limit_bytes=VMEM_LIMIT),
        cost_estimate=pl.CostEstimate(flops=1000, bytes_accessed=1000, transcendentals=0),
    )(*args)


def per_device(images, texts):
    rows, width = images.shape
    part = ((rows + EXTRA, width), (rows + EXTRA, width))
    part_text = ((rows, width), (rows, width))

    t_in = inward(texts)
    t_out = outward(texts)
    t_sib, i_sib = sibling(texts), sibling(images)
    i_in = inward(images)
    i_out = outward(images)
    t_far = across(t_in)
    i_far = across(i_in)

    i_mine, i_theirs = call(first_kernel, True, part, images, i_sib, texts, t_sib, t_in)
    i_mine, i_theirs = call(second_kernel, True, part, images, i_sib, t_out, i_mine, i_theirs)
    i_theirs = sibling(i_theirs)
    t_mine, t_theirs = call(first_kernel, False, part_text, texts, t_sib, images, i_sib, i_in)
    t_mine, t_theirs = call(second_kernel, False, part_text, texts, t_sib, i_out, t_mine, t_theirs)
    t_theirs = sibling(t_theirs)
    image_grad, pair_loss = call(last_kernel, True, ((rows, width), (1, rows)), images, t_far, i_mine, i_theirs)
    (text_grad,) = call(last_kernel, False, ((rows, width),), texts, i_far, t_mine, t_theirs)
    return (pair_loss.reshape(rows), image_grad, text_grad)


def solution(mesh):
    return jax.shard_map(
        per_device,
        mesh=mesh,
        in_specs=(P("blk", None), P("blk", None)),
        out_specs=(P("blk"), P("blk", None), P("blk", None)),
        check_vma=False,
    )
```

```python
import functools
import math

import jax
import jax.numpy as jnp
from jax import lax
from jax.experimental import pallas as pl
from jax.experimental.pallas import tpu as pltpu
from jax.sharding import PartitionSpec as P

CYCLE = 3
softness_factor = 2.0
logit_bias = -4.0
EXTRA = 8
FLOPS_C = 2_000_000_000
FLOPS_D = 2_000_000_000
VMEM_LIMIT = 24 * 1024 * 1024


def permuted(value, target):
    count = lax.axis_size("blk")
    return lax.ppermute(value, "blk", [(i, target(i) % count) for i in range(count)])


def sibling(value):
    return permuted(value, lambda i: i ^ 1)


def outward(value):
    return permuted(value, lambda i: i - 2 if i % 2 else i + 2)


def inward(value):
    return permuted(value, lambda i: i + 2 if i % 2 else i - 2)


def across(value):
    return permuted(value, lambda i: i + 1 if i % 2 else i - 1)


def after(value, *others):
    return lax.optimization_barrier((value,) + others)[0]


def halves(x):
    high = x.astype(jnp.bfloat16)
    return high, (x - high.astype(jnp.float32)).astype(jnp.bfloat16)


def dot(a, b, contract_b):
    dims = (((1,), (contract_b,)), ((), ()))
    return lax.dot_general(a, b, dims, preferred_element_type=jnp.float32)


def dots_of(own, block):
    return dot(own[0], block[0], 1) + dot(own[0], block[1], 1) + dot(own[1], block[0], 1)


def weighted(total, coefs, block):
    high, low = halves(coefs)
    first = dot(high, block[0], 0)
    total = first if total is None else total + first
    return total + dot(high, block[1], 0) + dot(low, block[0], 0)


def terms(own, block, positive=False, loss=False):
    scale = softness_factor / math.sqrt(own[0].shape[1])
    x = scale * dots_of(own, block) + logit_bias
    if positive:
        diagonal = lax.broadcasted_iota(jnp.int32, x.shape, 0) == lax.broadcasted_iota(jnp.int32, x.shape, 1)
        x = jnp.where(diagonal, -x, x)
    e = jnp.exp(-jnp.abs(x))
    r = 1.0 / (1.0 + e)
    coefs = jnp.where(x >= 0, r, e * r)
    if positive:
        coefs = jnp.where(diagonal, -coefs, coefs)
    if not loss:
        return coefs, None
    series = e * (1.0 - e * (0.5 - e * (1.0 / 3.0 - e * (0.25 - e * 0.2))))
    each = jnp.maximum(x, 0.0) + jnp.where(e < 0.0625, series, jnp.log(1.0 + e))
    return coefs, each[:, :128] + each[:, 128:]


def as_row(loss):
    return jnp.sum(loss.T, axis=0, keepdims=True)


def own_kernel(
    i_hbm, t_hbm, i_mine_ref, l_mine_ref, i_high_ref, i_low_ref, t_mine_ref, t_high_ref, t_low_ref, i_ref, t_ref, sems
):
    copies = [
        pltpu.make_async_copy(source, target, sems.at[k])
        for k, (source, target) in enumerate(((i_hbm, i_ref), (t_hbm, t_ref)))
    ]
    for copy in copies:
        copy.start()
    for copy in copies:
        copy.wait()
    own, texts = halves(i_ref[...]), halves(t_ref[...])
    i_high_ref[...], i_low_ref[...] = own
    t_high_ref[...], t_low_ref[...] = texts
    coefs, lost = terms(own, texts, True, True)
    i_mine_ref[...] = weighted(None, coefs, texts)
    l_mine_ref[...] = jnp.broadcast_to(as_row(lost), l_mine_ref.shape)
    coefs, _ = terms(texts, own, True)
    t_mine_ref[...] = weighted(None, coefs, own)


def texts_kernel(high_ref, low_ref, in_ref, out_ref, given_ref, l_given, mine_ref, l_mine_ref):
    own = high_ref[...], low_ref[...]
    blocks = [halves(in_ref[...]), halves(out_ref[...])]
    found = [terms(own, block, False, True) for block in blocks]
    mine = given_ref[...]
    for (coefs, _), block in zip(found, blocks):
        mine = weighted(mine, coefs, block)
    mine_ref[...] = mine
    l_mine_ref[...] = l_given[...] + as_row(found[0][1] + found[1][1])


def pair_kernel(
    i_sib_ref, t_sib_ref, in_ref, out_ref, i_high_ref, i_low_ref, t_high_ref, t_low_ref, i_given, l_given, t_given,
    i_mine_ref, theirs_ref, l_mine_ref, t_mine_ref, high_ref, low_ref,
):
    rows = i_sib_ref.shape[0]
    images, texts = halves(i_sib_ref[...]), halves(t_sib_ref[...])
    own_texts = t_high_ref[...], t_low_ref[...]
    high_ref[:rows, :], low_ref[:rows, :] = own_texts
    high_ref[rows:, :], low_ref[rows:, :] = texts
    coefs, lost = terms((i_high_ref[...], i_low_ref[...]), texts, False, True)
    i_mine_ref[...] = weighted(i_given[...], coefs, texts)
    l_mine_ref[...] = l_given[...] + as_row(lost)
    coefs, _ = terms(own_texts, images)
    t_mine_ref[...] = weighted(t_given[...], coefs, images)
    theirs, lost = None, 0.0
    for ref in (in_ref, out_ref):
        block = halves(ref[...])
        coefs, each = terms(images, block, False, True)
        theirs = weighted(theirs, coefs, block)
        lost = lost + each
    theirs_ref[:rows, :] = theirs
    theirs_ref[rows:, :rows] = jnp.broadcast_to(as_row(lost), (EXTRA, rows))


def images_kernel(high_ref, low_ref, in_ref, out_ref, given_ref, mine_ref, theirs_ref):
    rows = in_ref.shape[0]
    both = high_ref[...], low_ref[...]
    total = None
    blocks = [halves(in_ref[...]), halves(out_ref[...])]
    coefs = [terms(both, block)[0] for block in blocks]
    for coef, block in zip(coefs, blocks):
        total = weighted(total, coef, block)
    mine_ref[...] = given_ref[...] + total[:rows]
    theirs_ref[...] = total[rows:]


def far_kernel(loss, high_ref, low_ref, block_ref, given_ref, *rest):
    rows = block_ref.shape[0]
    block = halves(block_ref[...])
    coefs, each = terms((high_ref[:rows, :], low_ref[:rows, :]), block, False, loss)
    mine_ref = rest[1] if loss else rest[0]
    mine_ref[...] = weighted(given_ref[...], coefs, block)
    if loss:
        rest[2][...] = rest[0][...] + as_row(each)


def final_kernel(i_mine, i_theirs, l_mine, t_mine, t_theirs, image_ref, text_ref, loss_ref):
    rows, width = t_mine.shape
    scale = softness_factor / math.sqrt(width)
    image_ref[...] = scale * (i_mine[...] + i_theirs[:rows, :])
    text_ref[...] = scale * (t_mine[...] + t_theirs[...])
    loss_ref[...] = (l_mine[:1, :] + i_theirs[rows : rows + 1, :rows]) * (1.0 / ((2 * CYCLE + 1) * rows))


def call(kernel, outs, *args, flops=1000, **specs):
    return pl.pallas_call(
        kernel,
        out_shape=[jax.ShapeDtypeStruct(shape, dtype) for shape, dtype in outs],
        compiler_params=pltpu.CompilerParams(vmem_limit_bytes=VMEM_LIMIT),
        cost_estimate=pl.CostEstimate(flops=flops, bytes_accessed=1000, transcendentals=0),
        **specs,
    )(*args)


def per_device(images, texts):
    rows, width = images.shape
    f32, bf16 = jnp.float32, jnp.bfloat16
    grad, longer = ((rows, width), f32), ((rows + EXTRA, width), f32)
    low, low2, loss = ((rows, width), bf16), ((2 * rows, width), bf16), ((EXTRA, rows), f32)

    t_in, t_out = inward(texts), outward(texts)
    t_sib, i_sib = sibling(texts), sibling(images)
    i_mine, l_mine, i_high, i_low, t_mine, t_high, t_low = call(
        own_kernel,
        (grad, loss, low, low, grad, low, low),
        images,
        texts,
        in_specs=[pl.BlockSpec(memory_space=pl.ANY)] * 2,
        scratch_shapes=[pltpu.VMEM(images.shape, f32)] * 2 + [pltpu.SemaphoreType.DMA((2,))],
    )
    i_in, i_out = inward(after(images, t_mine)), outward(images)
    t_far = across(t_in)
    i_mine, l_mine = call(texts_kernel, (grad, loss), i_high, i_low, t_in, t_out, i_mine, l_mine)
    i_far = across(after(i_in, l_mine))
    i_mine, i_theirs, l_mine, t_mine, t_high, t_low = call(
        pair_kernel,
        (grad, longer, loss, grad, low2, low2),
        i_sib, t_sib, t_in, t_out, i_high, i_low, t_high, t_low, i_mine, l_mine, t_mine,
    )
    i_theirs = sibling(i_theirs)
    t_mine, t_theirs = call(images_kernel, (grad, grad), t_high, t_low, i_in, i_out, t_mine)
    t_theirs = sibling(t_theirs)
    i_mine, l_mine = call(
        functools.partial(far_kernel, True), (grad, loss), i_high, i_low, t_far, after(i_mine, t_mine), l_mine, flops=FLOPS_C
    )
    (t_mine,) = call(
        functools.partial(far_kernel, False), (grad,), t_high, t_low, i_far, after(t_mine, l_mine), flops=FLOPS_D
    )
    image_grad, text_grad, pair_loss = call(
        final_kernel, (grad, grad, ((1, rows), f32)), i_mine, i_theirs, l_mine, t_mine, t_theirs
    )
    return (pair_loss.reshape(rows), image_grad, text_grad)


def solution(mesh):
    return jax.shard_map(
        per_device,
        mesh=mesh,
        in_specs=(P("blk", None), P("blk", None)),
        out_specs=(P("blk"), P("blk", None), P("blk", None)),
        check_vma=False,
    )
```

```python
import functools
import math

import jax
import jax.numpy as jnp
from jax import lax
from jax.experimental import pallas as pl
from jax.experimental.pallas import tpu as pltpu
from jax.sharding import PartitionSpec as P

CYCLE = 3
softness_factor = 2.0
logit_bias = -4.0
EXTRA = 8
FLOPS_C = 2_000_000_000
FLOPS_D = 2_000_000_000
VMEM_LIMIT = 24 * 1024 * 1024


def permuted(value, target):
    count = lax.axis_size("blk")
    return lax.ppermute(value, "blk", [(i, target(i) % count) for i in range(count)])


def sibling(value):
    return permuted(value, lambda i: i ^ 1)


def outward(value):
    return permuted(value, lambda i: i - 2 if i % 2 else i + 2)


def inward(value):
    return permuted(value, lambda i: i + 2 if i % 2 else i - 2)


def across(value):
    return permuted(value, lambda i: i + 1 if i % 2 else i - 1)


def after(value, *others):
    return lax.optimization_barrier((value,) + others)[0]


def halves(x):
    high = x.astype(jnp.bfloat16)
    return high, (x - high.astype(jnp.float32)).astype(jnp.bfloat16)


def dot(a, b, contract_b):
    dims = (((1,), (contract_b,)), ((), ()))
    return lax.dot_general(a, b, dims, preferred_element_type=jnp.float32)


def dots_of(own, block):
    return dot(own[0], block[0], 1) + dot(own[0], block[1], 1) + dot(own[1], block[0], 1)


def weighted(total, coefs, block):
    high, low = halves(coefs)
    first = dot(high, block[0], 0)
    total = first if total is None else total + first
    return total + dot(high, block[1], 0) + dot(low, block[0], 0)


def terms(own, block, positive=False, loss=False):
    scale = softness_factor / math.sqrt(own[0].shape[1])
    x = scale * dots_of(own, block) + logit_bias
    if positive:
        diagonal = lax.broadcasted_iota(jnp.int32, x.shape, 0) == lax.broadcasted_iota(jnp.int32, x.shape, 1)
        x = jnp.where(diagonal, -x, x)
    e = jnp.exp(-jnp.abs(x))
    r = 1.0 / (1.0 + e)
    coefs = jnp.where(x >= 0, r, e * r)
    if positive:
        coefs = jnp.where(diagonal, -coefs, coefs)
    if not loss:
        return coefs, None
    series = e * (1.0 - e * (0.5 - e * (1.0 / 3.0 - e * (0.25 - e * 0.2))))
    each = jnp.maximum(x, 0.0) + jnp.where(e < 0.0625, series, jnp.log(1.0 + e))
    return coefs, each[:, :128] + each[:, 128:]


def as_row(loss):
    return jnp.sum(loss.T, axis=0, keepdims=True)


def own_kernel(
    i_hbm, t_hbm, first_ref, second_ref, i_mine_ref, l_mine_ref, i_high_ref, i_low_ref, t_mine_ref, t_high_ref, t_low_ref, i_ref, t_ref, sems
):
    copies = [
        pltpu.make_async_copy(source, target, sems.at[k])
        for k, (source, target) in enumerate(((i_hbm, i_ref), (t_hbm, t_ref)))
    ]
    for copy in copies:
        copy.start()
    for copy in copies:
        copy.wait()
    middle = first_ref.shape[0]
    first_ref[...], second_ref[...] = t_ref[:middle, :], t_ref[middle:, :]
    own, texts = halves(i_ref[...]), halves(t_ref[...])
    i_high_ref[...], i_low_ref[...] = own
    t_high_ref[...], t_low_ref[...] = texts
    coefs, lost = terms(own, texts, True, True)
    i_mine_ref[...] = weighted(None, coefs, texts)
    l_mine_ref[...] = jnp.broadcast_to(as_row(lost), l_mine_ref.shape)
    coefs, _ = terms(texts, own, True)
    t_mine_ref[...] = weighted(None, coefs, own)


def texts_kernel(
    i_high_ref, i_low_ref, t_high_ref, t_low_ref, i_sib_ref, in_ref, out_ref, i_given, l_given, t_given,
    i_mine_ref, l_mine_ref, t_mine_ref, high_ref, low_ref,
):
    own, texts, images = (i_high_ref[...], i_low_ref[...]), (t_high_ref[...], t_low_ref[...]), halves(i_sib_ref[...])
    high_ref[...], low_ref[...] = images
    blocks = [halves(in_ref[...]), halves(out_ref[...])]
    found = [terms(own, block, False, True) for block in blocks]
    coefs, _ = terms(texts, images)
    t_mine_ref[...] = weighted(t_given[...], coefs, images)
    mine = i_given[...]
    for (coefs, _), block in zip(found, blocks):
        mine = weighted(mine, coefs, block)
    i_mine_ref[...] = mine
    l_mine_ref[...] = l_given[...] + as_row(found[0][1] + found[1][1])


def pair_kernel(
    i_sib_high, i_sib_low, t_sib_first, t_sib_second, in_ref, out_ref, i_high_ref, i_low_ref, t_high_ref, t_low_ref, i_given, l_given,
    i_mine_ref, theirs_ref, l_mine_ref, high_ref, low_ref,
):
    rows = in_ref.shape[0]
    images, texts = (i_sib_high[...], i_sib_low[...]), halves(jnp.concatenate([t_sib_first[...], t_sib_second[...]]))
    high_ref[:rows, :], low_ref[:rows, :] = t_high_ref[...], t_low_ref[...]
    high_ref[rows:, :], low_ref[rows:, :] = texts
    blocks = [halves(in_ref[...]), halves(out_ref[...])]
    coefs, lost = terms((i_high_ref[...], i_low_ref[...]), texts, False, True)
    found = [terms(images, block, False, True) for block in blocks]
    i_mine_ref[...] = weighted(i_given[...], coefs, texts)
    l_mine_ref[...] = l_given[...] + as_row(lost)
    theirs = None
    for (coefs, _), block in zip(found, blocks):
        theirs = weighted(theirs, coefs, block)
    theirs_ref[:rows, :] = theirs
    theirs_ref[rows:, :rows] = jnp.broadcast_to(as_row(found[0][1] + found[1][1]), (EXTRA, rows))


def images_kernel(high_ref, low_ref, in_ref, out_ref, given_ref, mine_ref, theirs_ref):
    rows = in_ref.shape[0]
    both = high_ref[...], low_ref[...]
    total = None
    blocks = [halves(in_ref[...]), halves(out_ref[...])]
    coefs = [terms(both, block)[0] for block in blocks]
    for coef, block in zip(coefs, blocks):
        total = weighted(total, coef, block)
    mine_ref[...] = given_ref[...] + total[:rows]
    theirs_ref[...] = total[rows:]


def far_kernel(loss, high_ref, low_ref, block_ref, given_ref, *rest):
    rows = block_ref.shape[0]
    block = halves(block_ref[...])
    coefs, each = terms((high_ref[:rows, :], low_ref[:rows, :]), block, False, loss)
    mine_ref = rest[1] if loss else rest[0]
    mine_ref[...] = weighted(given_ref[...], coefs, block)
    if loss:
        rest[2][...] = rest[0][...] + as_row(each)


def final_kernel(i_mine, i_theirs, l_mine, t_mine, t_theirs, image_ref, text_ref, loss_ref):
    rows, width = t_mine.shape
    scale = softness_factor / math.sqrt(width)
    image_ref[...] = scale * (i_mine[...] + i_theirs[:rows, :])
    text_ref[...] = scale * (t_mine[...] + t_theirs[...])
    loss_ref[...] = (l_mine[:1, :] + i_theirs[rows : rows + 1, :rows]) * (1.0 / ((2 * CYCLE + 1) * rows))


def call(kernel, outs, *args, flops=1000, **specs):
    return pl.pallas_call(
        kernel,
        out_shape=[jax.ShapeDtypeStruct(shape, dtype) for shape, dtype in outs],
        compiler_params=pltpu.CompilerParams(vmem_limit_bytes=VMEM_LIMIT),
        cost_estimate=pl.CostEstimate(flops=flops, bytes_accessed=1000, transcendentals=0),
        **specs,
    )(*args)


def per_device(images, texts):
    rows, width = images.shape
    f32, bf16 = jnp.float32, jnp.bfloat16
    grad, longer = ((rows, width), f32), ((rows + EXTRA, width), f32)
    half = ((rows // 2, width), f32)
    low, low2, loss = ((rows, width), bf16), ((2 * rows, width), bf16), ((EXTRA, rows), f32)

    t_in, t_out = inward(texts), outward(texts)
    i_sib = sibling(images)
    *t_parts, i_mine, l_mine, i_high, i_low, t_mine, t_high, t_low = call(
        own_kernel,
        (half, half, grad, loss, low, low, grad, low, low),
        images,
        texts,
        in_specs=[pl.BlockSpec(memory_space=pl.ANY)] * 2,
        scratch_shapes=[pltpu.VMEM(images.shape, f32)] * 2 + [pltpu.SemaphoreType.DMA((2,))],
    )
    i_in, i_out = inward(after(images, t_mine)), outward(images)
    t_far = across(t_in)
    i_mine, l_mine, t_mine, i_sib_high, i_sib_low = call(
        texts_kernel,
        (grad, loss, grad, low, low),
        i_high, i_low, t_high, t_low, i_sib, t_in, t_out, i_mine, l_mine, t_mine,
    )
    i_far = across(after(i_in, l_mine))
    t_sib = [sibling(after(part, l_mine)) for part in t_parts]
    i_mine, i_theirs, l_mine, t_high, t_low = call(
        pair_kernel,
        (grad, longer, loss, low2, low2),
        i_sib_high, i_sib_low, *t_sib, t_in, t_out, i_high, i_low, t_high, t_low, i_mine, l_mine,
    )
    i_theirs = sibling(i_theirs)
    t_mine, t_theirs = call(images_kernel, (grad, grad), t_high, t_low, i_in, i_out, t_mine)
    t_theirs = sibling(t_theirs)
    i_mine, l_mine = call(
        functools.partial(far_kernel, True), (grad, loss), i_high, i_low, t_far, after(i_mine, t_mine), l_mine, flops=FLOPS_C
    )
    (t_mine,) = call(
        functools.partial(far_kernel, False), (grad,), t_high, t_low, i_far, after(t_mine, l_mine), flops=FLOPS_D
    )
    image_grad, text_grad, pair_loss = call(
        final_kernel, (grad, grad, ((1, rows), f32)), i_mine, i_theirs, l_mine, t_mine, t_theirs
    )
    return (pair_loss.reshape(rows), image_grad, text_grad)


def solution(mesh):
    return jax.shard_map(
        per_device,
        mesh=mesh,
        in_specs=(P("blk", None), P("blk", None)),
        out_specs=(P("blk"), P("blk", None), P("blk", None)),
        check_vma=False,
    )
```

```python
import functools
import math

import jax
import jax.numpy as jnp
from jax import lax
from jax.experimental import pallas as pl
from jax.experimental.pallas import tpu as pltpu
from jax.sharding import PartitionSpec as P

CYCLE = 3
softness_factor = 2.0
logit_bias = -4.0
EXTRA = 8
FLOPS_C = 1_000_000_000
FLOPS_D = 10_000_000_000
VMEM_LIMIT = 24 * 1024 * 1024


def permuted(value, target):
    count = lax.axis_size("blk")
    return lax.ppermute(value, "blk", [(i, target(i) % count) for i in range(count)])


def sibling(value):
    return permuted(value, lambda i: i ^ 1)


def outward(value):
    return permuted(value, lambda i: i - 2 if i % 2 else i + 2)


def inward(value):
    return permuted(value, lambda i: i + 2 if i % 2 else i - 2)


def across(value):
    return permuted(value, lambda i: i + 1 if i % 2 else i - 1)


def after(value, *others):
    return lax.optimization_barrier((value,) + others)[0]


def halves(x):
    high = x.astype(jnp.bfloat16)
    return high, (x - high.astype(jnp.float32)).astype(jnp.bfloat16)


def dot(a, b, contract_b):
    dims = (((1,), (contract_b,)), ((), ()))
    return lax.dot_general(a, b, dims, preferred_element_type=jnp.float32)


def dots_of(own, block):
    return dot(own[0], block[0], 1) + dot(own[0], block[1], 1) + dot(own[1], block[0], 1)


def weighted(total, coefs, block):
    high, low = halves(coefs)
    first = dot(high, block[0], 0)
    total = first if total is None else total + first
    return total + dot(high, block[1], 0) + dot(low, block[0], 0)


def terms(own, block, positive=False, loss=False):
    scale = softness_factor / math.sqrt(own[0].shape[1])
    x = scale * dots_of(own, block) + logit_bias
    if positive:
        diagonal = lax.broadcasted_iota(jnp.int32, x.shape, 0) == lax.broadcasted_iota(jnp.int32, x.shape, 1)
        x = jnp.where(diagonal, -x, x)
    e = jnp.exp(-jnp.abs(x))
    r = 1.0 / (1.0 + e)
    coefs = jnp.where(x >= 0, r, e * r)
    if positive:
        coefs = jnp.where(diagonal, -coefs, coefs)
    if not loss:
        return coefs, None
    series = e * (1.0 - e * (0.5 - e * (1.0 / 3.0 - e * (0.25 - e * 0.2))))
    each = jnp.maximum(x, 0.0) + jnp.where(e < 0.0625, series, jnp.log(1.0 + e))
    return coefs, each[:, :128] + each[:, 128:]


def as_row(loss):
    return jnp.sum(loss.T, axis=0, keepdims=True)


def own_kernel(
    i_hbm, t_hbm, first_ref, second_ref, i_mine_ref, l_mine_ref, i_high_ref, i_low_ref, t_mine_ref, t_high_ref, t_low_ref, i_ref, t_ref, sems
):
    copies = [
        pltpu.make_async_copy(source, target, sems.at[k])
        for k, (source, target) in enumerate(((i_hbm, i_ref), (t_hbm, t_ref)))
    ]
    for copy in copies:
        copy.start()
    for copy in copies:
        copy.wait()
    middle = first_ref.shape[0]
    first_ref[...], second_ref[...] = t_ref[:middle, :], t_ref[middle:, :]
    own, texts = halves(i_ref[...]), halves(t_ref[...])
    i_high_ref[...], i_low_ref[...] = own
    t_high_ref[...], t_low_ref[...] = texts
    coefs, lost = terms(own, texts, True, True)
    i_mine_ref[...] = weighted(None, coefs, texts)
    l_mine_ref[...] = jnp.broadcast_to(as_row(lost), l_mine_ref.shape)
    coefs, _ = terms(texts, own, True)
    t_mine_ref[...] = weighted(None, coefs, own)


def texts_kernel(
    i_high_ref, i_low_ref, t_high_ref, t_low_ref, i_sib_ref, in_ref, out_ref, i_given, l_given, t_given,
    i_mine_ref, l_mine_ref, t_mine_ref, high_ref, low_ref,
):
    own, texts, images = (i_high_ref[...], i_low_ref[...]), (t_high_ref[...], t_low_ref[...]), halves(i_sib_ref[...])
    high_ref[...], low_ref[...] = images
    blocks = [halves(in_ref[...]), halves(out_ref[...])]
    found = [terms(own, block, False, True) for block in blocks]
    coefs, _ = terms(texts, images)
    t_mine_ref[...] = weighted(t_given[...], coefs, images)
    mine = i_given[...]
    for (coefs, _), block in zip(found, blocks):
        mine = weighted(mine, coefs, block)
    i_mine_ref[...] = mine
    l_mine_ref[...] = l_given[...] + as_row(found[0][1] + found[1][1])


def pair_kernel(
    i_sib_high, i_sib_low, t_sib_first, t_sib_second, in_ref, out_ref, i_high_ref, i_low_ref, t_high_ref, t_low_ref, i_given, l_given,
    i_mine_ref, theirs_ref, l_mine_ref, high_ref, low_ref,
):
    rows = in_ref.shape[0]
    images, texts = (i_sib_high[...], i_sib_low[...]), halves(jnp.concatenate([t_sib_first[...], t_sib_second[...]]))
    high_ref[:rows, :], low_ref[:rows, :] = t_high_ref[...], t_low_ref[...]
    high_ref[rows:, :], low_ref[rows:, :] = texts
    blocks = [halves(in_ref[...]), halves(out_ref[...])]
    coefs, lost = terms((i_high_ref[...], i_low_ref[...]), texts, False, True)
    found = [terms(images, block, False, True) for block in blocks]
    i_mine_ref[...] = weighted(i_given[...], coefs, texts)
    l_mine_ref[...] = l_given[...] + as_row(lost)
    theirs = None
    for (coefs, _), block in zip(found, blocks):
        theirs = weighted(theirs, coefs, block)
    theirs_ref[:rows, :] = theirs
    theirs_ref[rows:, :rows] = jnp.broadcast_to(as_row(found[0][1] + found[1][1]), (EXTRA, rows))


def images_kernel(high_ref, low_ref, in_ref, out_ref, given_ref, i_theirs_ref, mine_ref, theirs_ref):
    rows = in_ref.shape[0]
    both = high_ref[...], low_ref[...]
    total = None
    blocks = [halves(in_ref[...]), halves(out_ref[...])]
    coefs = [terms(both, block)[0] for block in blocks]
    for coef, block in zip(coefs, blocks):
        total = weighted(total, coef, block)
    mine_ref[...] = given_ref[...] + total[:rows]
    theirs_ref[:rows, :] = total[rows:]
    theirs_ref[rows:, :] = i_theirs_ref[...]


def far_texts_kernel(high_ref, low_ref, block_ref, given_ref, l_given, mine_ref, l_mine_ref):
    block = halves(block_ref[...])
    coefs, each = terms((high_ref[...], low_ref[...]), block, False, True)
    mine_ref[...] = weighted(given_ref[...], coefs, block)
    l_mine_ref[...] = l_given[...] + as_row(each)


def far_images_kernel(high_ref, low_ref, block_ref, c_high_ref, c_low_ref, b_high_ref, b_low_ref):
    rows = block_ref.shape[0]
    block = halves(block_ref[...])
    b_high_ref[...], b_low_ref[...] = block
    coefs, _ = terms((high_ref[:rows, :], low_ref[:rows, :]), block)
    c_high_ref[...], c_low_ref[...] = halves(coefs)


def last_kernel(
    c_high_ref, c_low_ref, b_high_ref, b_low_ref, i_mine, t_mine, l_mine, theirs, image_ref, text_ref, loss_ref
):
    rows, width = t_mine.shape
    scale = softness_factor / math.sqrt(width)
    image_ref[...] = scale * (i_mine[...] + theirs[rows : 2 * rows, :])
    loss_ref[...] = (l_mine[:1, :] + theirs[2 * rows : 2 * rows + 1, :rows]) * (1.0 / ((2 * CYCLE + 1) * rows))
    high, low, b_high = c_high_ref[...], c_low_ref[...], b_high_ref[...]
    total = dot(high, b_high, 0) + dot(high, b_low_ref[...], 0) + dot(low, b_high, 0)
    text_ref[...] = scale * (total + (t_mine[...] + theirs[:rows, :]))


def call(kernel, outs, *args, flops=1000, **specs):
    return pl.pallas_call(
        kernel,
        out_shape=[jax.ShapeDtypeStruct(shape, dtype) for shape, dtype in outs],
        compiler_params=pltpu.CompilerParams(vmem_limit_bytes=VMEM_LIMIT),
        cost_estimate=pl.CostEstimate(flops=flops, bytes_accessed=1000, transcendentals=0),
        **specs,
    )(*args)


def per_device(images, texts):
    rows, width = images.shape
    f32, bf16 = jnp.float32, jnp.bfloat16
    grad, longer = ((rows, width), f32), ((rows + EXTRA, width), f32)
    half = ((rows // 2, width), f32)
    low, low2, loss = ((rows, width), bf16), ((2 * rows, width), bf16), ((EXTRA, rows), f32)

    t_in, t_out = inward(texts), outward(texts)
    i_sib = sibling(images)
    *t_parts, i_mine, l_mine, i_high, i_low, t_mine, t_high, t_low = call(
        own_kernel,
        (half, half, grad, loss, low, low, grad, low, low),
        images,
        texts,
        in_specs=[pl.BlockSpec(memory_space=pl.ANY)] * 2,
        scratch_shapes=[pltpu.VMEM(images.shape, f32)] * 2 + [pltpu.SemaphoreType.DMA((2,))],
    )
    i_in, i_out = inward(after(images, t_mine)), outward(images)
    t_far = across(t_in)
    i_mine, l_mine, t_mine, i_sib_high, i_sib_low = call(
        texts_kernel,
        (grad, loss, grad, low, low),
        i_high, i_low, t_high, t_low, i_sib, t_in, t_out, i_mine, l_mine, t_mine,
    )
    i_far = across(after(i_in, l_mine))
    t_sib = [sibling(after(part, l_mine)) for part in t_parts]
    i_mine, i_theirs, l_mine, t_high, t_low = call(
        pair_kernel,
        (grad, longer, loss, low2, low2),
        i_sib_high, i_sib_low, *t_sib, t_in, t_out, i_high, i_low, t_high, t_low, i_mine, l_mine,
    )
    t_mine, theirs = call(
        images_kernel, (grad, ((2 * rows + EXTRA, width), f32)), t_high, t_low, i_in, i_out, t_mine, i_theirs
    )
    i_mine, l_mine = call(
        far_texts_kernel, (grad, loss), i_high, i_low, t_far, after(i_mine, t_mine), l_mine, flops=FLOPS_C
    )
    theirs = sibling(theirs)
    square = ((rows, rows), bf16)
    found = call(far_images_kernel, (square, square, low, low), t_high, after(t_low, l_mine), i_far, flops=FLOPS_D)
    image_grad, text_grad, pair_loss = call(
        last_kernel, (grad, grad, ((1, rows), f32)), *found, i_mine, t_mine, l_mine, theirs
    )
    return (pair_loss.reshape(rows), image_grad, text_grad)


def solution(mesh):
    return jax.shard_map(
        per_device,
        mesh=mesh,
        in_specs=(P("blk", None), P("blk", None)),
        out_specs=(P("blk"), P("blk", None), P("blk", None)),
        check_vma=False,
    )
```

```python
import functools
import math

import jax
import jax.numpy as jnp
from jax import lax
from jax.experimental import pallas as pl
from jax.experimental.pallas import tpu as pltpu
from jax.sharding import PartitionSpec as P

CYCLE = 3
softness_factor = 2.0
logit_bias = -4.0
EXTRA = 8
FLOPS_C = 1_000_000_000
FLOPS_D = 10_000_000_000
VMEM_LIMIT = 24 * 1024 * 1024


def permuted(value, target):
    count = lax.axis_size("blk")
    return lax.ppermute(value, "blk", [(i, target(i) % count) for i in range(count)])


def sibling(value):
    return permuted(value, lambda i: i ^ 1)


def outward(value):
    return permuted(value, lambda i: i - 2 if i % 2 else i + 2)


def inward(value):
    return permuted(value, lambda i: i + 2 if i % 2 else i - 2)


def across(value):
    return permuted(value, lambda i: i + 1 if i % 2 else i - 1)


def after(value, *others):
    return lax.optimization_barrier((value,) + others)[0]


def halves(x):
    high = x.astype(jnp.bfloat16)
    return high, (x - high.astype(jnp.float32)).astype(jnp.bfloat16)


def dot(a, b, contract_b):
    dims = (((1,), (contract_b,)), ((), ()))
    return lax.dot_general(a, b, dims, preferred_element_type=jnp.float32)


def dots_of(own, block):
    return dot(own[0], block[0], 1) + dot(own[0], block[1], 1) + dot(own[1], block[0], 1)


def weighted(total, coefs, block):
    high, low = halves(coefs)
    first = dot(high, block[0], 0)
    total = first if total is None else total + first
    return total + dot(high, block[1], 0) + dot(low, block[0], 0)


def terms(own, block, positive=False, loss=False):
    scale = softness_factor / math.sqrt(own[0].shape[1])
    x = scale * dots_of(own, block) + logit_bias
    if positive:
        diagonal = lax.broadcasted_iota(jnp.int32, x.shape, 0) == lax.broadcasted_iota(jnp.int32, x.shape, 1)
        x = jnp.where(diagonal, -x, x)
    e = jnp.exp(-jnp.abs(x))
    r = 1.0 / (1.0 + e)
    coefs = jnp.where(x >= 0, r, e * r)
    if positive:
        coefs = jnp.where(diagonal, -coefs, coefs)
    if not loss:
        return coefs, None
    series = e * (1.0 - e * (0.5 - e * (1.0 / 3.0 - e * (0.25 - e * 0.2))))
    each = jnp.maximum(x, 0.0) + jnp.where(e < 0.0625, series, jnp.log(1.0 + e))
    return coefs, each[:, :128] + each[:, 128:]


def as_row(loss):
    return jnp.sum(loss.T, axis=0, keepdims=True)


def own_kernel(
    i_hbm, t_hbm, first_ref, second_ref, i_mine_ref, l_mine_ref, i_high_ref, i_low_ref, t_high_ref, t_low_ref, i_ref, t_ref, sems
):
    copies = [
        pltpu.make_async_copy(source, target, sems.at[k])
        for k, (source, target) in enumerate(((i_hbm, i_ref), (t_hbm, t_ref)))
    ]
    for copy in copies:
        copy.start()
    for copy in copies:
        copy.wait()
    middle = first_ref.shape[0]
    first_ref[...], second_ref[...] = t_ref[:middle, :], t_ref[middle:, :]
    own, texts = halves(i_ref[...]), halves(t_ref[...])
    i_high_ref[...], i_low_ref[...] = own
    t_high_ref[...], t_low_ref[...] = texts
    coefs, lost = terms(own, texts, True, True)
    i_mine_ref[...] = weighted(None, coefs, texts)
    l_mine_ref[...] = jnp.broadcast_to(as_row(lost), l_mine_ref.shape)


def texts_kernel(
    i_high_ref, i_low_ref, t_high_ref, t_low_ref, in_ref, out_ref, i_sib_ref, i_given, l_given,
    i_mine_ref, l_mine_ref, t_mine_ref, high_ref, low_ref,
):
    own, texts, images = (i_high_ref[...], i_low_ref[...]), (t_high_ref[...], t_low_ref[...]), halves(i_sib_ref[...])
    high_ref[...], low_ref[...] = images
    blocks = [halves(in_ref[...]), halves(out_ref[...])]
    found = [terms(own, block, False, True) for block in blocks]
    coefs, _ = terms(texts, images)
    t_mine_ref[...] = weighted(None, coefs, images)
    mine = i_given[...]
    for (coefs, _), block in zip(found, blocks):
        mine = weighted(mine, coefs, block)
    i_mine_ref[...] = mine
    l_mine_ref[...] = l_given[...] + as_row(found[0][1] + found[1][1])


def pair_kernel(
    i_sib_high, i_sib_low, t_sib_first, t_sib_second, in_ref, out_ref, i_high_ref, i_low_ref, t_high_ref, t_low_ref, i_given, l_given,
    i_mine_ref, theirs_ref, l_mine_ref, high_ref, low_ref,
):
    rows = in_ref.shape[0]
    images, texts = (i_sib_high[...], i_sib_low[...]), halves(jnp.concatenate([t_sib_first[...], t_sib_second[...]]))
    high_ref[:rows, :], low_ref[:rows, :] = t_high_ref[...], t_low_ref[...]
    high_ref[rows:, :], low_ref[rows:, :] = texts
    blocks = [halves(in_ref[...]), halves(out_ref[...])]
    coefs, lost = terms((i_high_ref[...], i_low_ref[...]), texts, False, True)
    found = [terms(images, block, False, True) for block in blocks]
    i_mine_ref[...] = weighted(i_given[...], coefs, texts)
    l_mine_ref[...] = l_given[...] + as_row(lost)
    theirs = None
    for (coefs, _), block in zip(found, blocks):
        theirs = weighted(theirs, coefs, block)
    theirs_ref[:rows, :] = theirs
    theirs_ref[rows:, :rows] = jnp.broadcast_to(as_row(found[0][1] + found[1][1]), (EXTRA, rows))


def images_kernel(high_ref, low_ref, in_ref, out_ref, given_ref, i_theirs_ref, mine_ref, theirs_ref):
    rows = in_ref.shape[0]
    both = high_ref[...], low_ref[...]
    total = None
    blocks = [halves(in_ref[...]), halves(out_ref[...])]
    coefs = [terms(both, block)[0] for block in blocks]
    for coef, block in zip(coefs, blocks):
        total = weighted(total, coef, block)
    mine_ref[...] = given_ref[...] + total[:rows]
    theirs_ref[:rows, :] = total[rows:]
    theirs_ref[rows:, :] = i_theirs_ref[...]


def far_texts_kernel(
    i_high_ref, i_low_ref, t_high_ref, t_low_ref, block_ref, i_given, l_given, t_given, i_mine_ref, l_mine_ref, t_mine_ref
):
    rows = block_ref.shape[0]
    own, texts, block = (i_high_ref[...], i_low_ref[...]), (t_high_ref[:rows, :], t_low_ref[:rows, :]), halves(block_ref[...])
    coefs, each = terms(own, block, False, True)
    i_mine_ref[...] = weighted(i_given[...], coefs, block)
    l_mine_ref[...] = l_given[...] + as_row(each)
    coefs, _ = terms(texts, own, True)
    t_mine_ref[...] = weighted(t_given[...], coefs, own)


def far_images_kernel(high_ref, low_ref, block_ref, c_high_ref, c_low_ref, b_high_ref, b_low_ref):
    rows = block_ref.shape[0]
    block = halves(block_ref[...])
    b_high_ref[...], b_low_ref[...] = block
    coefs, _ = terms((high_ref[:rows, :], low_ref[:rows, :]), block)
    c_high_ref[...], c_low_ref[...] = halves(coefs)


def last_kernel(
    c_high_ref, c_low_ref, b_high_ref, b_low_ref, i_mine, t_mine, l_mine, theirs, image_ref, text_ref, loss_ref
):
    rows, width = t_mine.shape
    scale = softness_factor / math.sqrt(width)
    image_ref[...] = scale * (i_mine[...] + theirs[rows : 2 * rows, :])
    loss_ref[...] = (l_mine[:1, :] + theirs[2 * rows : 2 * rows + 1, :rows]) * (1.0 / ((2 * CYCLE + 1) * rows))
    high, low, b_high = c_high_ref[...], c_low_ref[...], b_high_ref[...]
    total = dot(high, b_high, 0) + dot(high, b_low_ref[...], 0) + dot(low, b_high, 0)
    text_ref[...] = scale * (total + (t_mine[...] + theirs[:rows, :]))


def call(kernel, outs, *args, flops=1000, **specs):
    return pl.pallas_call(
        kernel,
        out_shape=[jax.ShapeDtypeStruct(shape, dtype) for shape, dtype in outs],
        compiler_params=pltpu.CompilerParams(vmem_limit_bytes=VMEM_LIMIT),
        cost_estimate=pl.CostEstimate(flops=flops, bytes_accessed=1000, transcendentals=0),
        **specs,
    )(*args)


def per_device(images, texts):
    rows, width = images.shape
    f32, bf16 = jnp.float32, jnp.bfloat16
    grad, longer = ((rows, width), f32), ((rows + EXTRA, width), f32)
    half = ((rows // 2, width), f32)
    low, low2, loss = ((rows, width), bf16), ((2 * rows, width), bf16), ((EXTRA, rows), f32)

    t_in, t_out = inward(texts), outward(texts)
    i_sib = sibling(images)
    *t_parts, i_mine, l_mine, i_high, i_low, t_high, t_low = call(
        own_kernel,
        (half, half, grad, loss, low, low, low, low),
        images,
        texts,
        in_specs=[pl.BlockSpec(memory_space=pltpu.HBM)] * 2,
        scratch_shapes=[pltpu.VMEM(images.shape, f32)] * 2 + [pltpu.SemaphoreType.DMA((2,))],
    )
    i_in, i_out = inward(after(images, l_mine)), outward(images)
    t_far = across(t_in)
    i_mine, l_mine, t_mine, i_sib_high, i_sib_low = call(
        texts_kernel,
        (grad, loss, grad, low, low),
        i_high, i_low, t_high, t_low, t_in, t_out, i_sib, i_mine, l_mine,
    )
    i_far = across(after(i_in, l_mine))
    t_sib = [sibling(after(part, l_mine)) for part in t_parts]
    i_mine, i_theirs, l_mine, t_high, t_low = call(
        pair_kernel,
        (grad, longer, loss, low2, low2),
        i_sib_high, i_sib_low, *t_sib, t_in, t_out, i_high, i_low, t_high, t_low, i_mine, l_mine,
    )
    t_mine, theirs = call(
        images_kernel, (grad, ((2 * rows + EXTRA, width), f32)), t_high, t_low, i_in, i_out, t_mine, i_theirs
    )
    i_mine, l_mine, t_mine = call(
        far_texts_kernel, (grad, loss, grad), i_high, i_low, t_high, t_low, t_far, i_mine, l_mine, t_mine, flops=FLOPS_C
    )
    theirs = sibling(theirs)
    square = ((rows, rows), bf16)
    found = call(far_images_kernel, (square, square, low, low), t_high, after(t_low, l_mine), i_far, flops=FLOPS_D)
    image_grad, text_grad, pair_loss = call(
        last_kernel, (grad, grad, ((1, rows), f32)), *found, i_mine, t_mine, l_mine, theirs
    )
    return (pair_loss.reshape(rows), image_grad, text_grad)


def solution(mesh):
    return jax.shard_map(
        per_device,
        mesh=mesh,
        in_specs=(P("blk", None), P("blk", None)),
        out_specs=(P("blk"), P("blk", None), P("blk", None)),
        check_vma=False,
    )
```

```python
import functools
import math

import jax
import jax.numpy as jnp
from jax import lax
from jax.experimental import pallas as pl
from jax.experimental.pallas import tpu as pltpu
from jax.sharding import PartitionSpec as P

CYCLE = 3
softness_factor = 2.0
logit_bias = -4.0
EXTRA = 8
FLOPS_C = 2_000_000_000
FLOPS_D = 10_000_000_000
VMEM_LIMIT = 24 * 1024 * 1024


def permuted(value, target):
    count = lax.axis_size("blk")
    return lax.ppermute(value, "blk", [(i, target(i) % count) for i in range(count)])


def sibling(value):
    return permuted(value, lambda i: i ^ 1)


def outward(value):
    return permuted(value, lambda i: i - 2 if i % 2 else i + 2)


def inward(value):
    return permuted(value, lambda i: i + 2 if i % 2 else i - 2)


def across(value):
    return permuted(value, lambda i: i + 1 if i % 2 else i - 1)


def after(value, *others):
    return lax.optimization_barrier((value,) + others)[0]


def halves(x):
    high = x.astype(jnp.bfloat16)
    return high, (x - high.astype(jnp.float32)).astype(jnp.bfloat16)


def dot(a, b, contract_b):
    dims = (((1,), (contract_b,)), ((), ()))
    return lax.dot_general(a, b, dims, preferred_element_type=jnp.float32)


def dots_of(own, block):
    return dot(own[0], block[0], 1) + dot(own[0], block[1], 1) + dot(own[1], block[0], 1)


def weighted(total, coefs, block):
    high, low = halves(coefs)
    first = dot(high, block[0], 0)
    total = first if total is None else total + first
    return total + dot(high, block[1], 0) + dot(low, block[0], 0)


def terms(own, block, positive=False, loss=False):
    scale = softness_factor / math.sqrt(own[0].shape[1])
    x = scale * dots_of(own, block) + logit_bias
    if positive:
        diagonal = lax.broadcasted_iota(jnp.int32, x.shape, 0) == lax.broadcasted_iota(jnp.int32, x.shape, 1)
        x = jnp.where(diagonal, -x, x)
    e = jnp.exp(-jnp.abs(x))
    r = 1.0 / (1.0 + e)
    coefs = jnp.where(x >= 0, r, e * r)
    if positive:
        coefs = jnp.where(diagonal, -coefs, coefs)
    if not loss:
        return coefs, None
    series = e * (1.0 - e * (0.5 - e * (1.0 / 3.0 - e * (0.25 - e * 0.2))))
    each = jnp.maximum(x, 0.0) + jnp.where(e < 0.0625, series, jnp.log(1.0 + e))
    return coefs, each[:, :128] + each[:, 128:]


def as_row(loss):
    return jnp.sum(loss.T, axis=0, keepdims=True)


def own_kernel(
    i_hbm, t_hbm, first_ref, second_ref, i_mine_ref, l_mine_ref, i_high_ref, i_low_ref, t_high_ref, t_low_ref, i_ref, t_ref, sems
):
    copies = [
        pltpu.make_async_copy(source, target, sems.at[k])
        for k, (source, target) in enumerate(((i_hbm, i_ref), (t_hbm, t_ref)))
    ]
    for copy in copies:
        copy.start()
    for copy in copies:
        copy.wait()
    middle = first_ref.shape[0]
    first_ref[...], second_ref[...] = t_ref[:middle, :], t_ref[middle:, :]
    own, texts = halves(i_ref[...]), halves(t_ref[...])
    i_high_ref[...], i_low_ref[...] = own
    t_high_ref[...], t_low_ref[...] = texts
    coefs, lost = terms(own, texts, True, True)
    i_mine_ref[...] = weighted(None, coefs, texts)
    l_mine_ref[...] = jnp.broadcast_to(as_row(lost), l_mine_ref.shape)


def texts_kernel(
    i_high_ref, i_low_ref, t_high_ref, t_low_ref, in_ref, out_ref, i_sib_ref, i_given, l_given,
    i_mine_ref, l_mine_ref, t_mine_ref, high_ref, low_ref,
):
    own, texts, images = (i_high_ref[...], i_low_ref[...]), (t_high_ref[...], t_low_ref[...]), halves(i_sib_ref[...])
    high_ref[...], low_ref[...] = images
    blocks = [halves(in_ref[...]), halves(out_ref[...])]
    found = [terms(own, block, False, True) for block in blocks]
    coefs, _ = terms(texts, images)
    t_mine_ref[...] = weighted(None, coefs, images)
    mine = i_given[...]
    for (coefs, _), block in zip(found, blocks):
        mine = weighted(mine, coefs, block)
    i_mine_ref[...] = mine
    l_mine_ref[...] = l_given[...] + as_row(found[0][1] + found[1][1])


def pair_kernel(
    i_sib_high, i_sib_low, t_sib_first, t_sib_second, in_ref, out_ref, i_high_ref, i_low_ref, t_high_ref, t_low_ref, i_given, l_given,
    i_mine_ref, theirs_ref, l_mine_ref, high_ref, low_ref,
):
    rows = in_ref.shape[0]
    images, texts = (i_sib_high[...], i_sib_low[...]), halves(jnp.concatenate([t_sib_first[...], t_sib_second[...]]))
    high_ref[:rows, :], low_ref[:rows, :] = t_high_ref[...], t_low_ref[...]
    high_ref[rows:, :], low_ref[rows:, :] = texts
    blocks = [halves(in_ref[...]), halves(out_ref[...])]
    coefs, lost = terms((i_high_ref[...], i_low_ref[...]), texts, False, True)
    found = [terms(images, block, False, True) for block in blocks]
    i_mine_ref[...] = weighted(i_given[...], coefs, texts)
    l_mine_ref[...] = l_given[...] + as_row(lost)
    theirs = None
    for (coefs, _), block in zip(found, blocks):
        theirs = weighted(theirs, coefs, block)
    theirs_ref[:rows, :] = theirs
    theirs_ref[rows:, :rows] = jnp.broadcast_to(as_row(found[0][1] + found[1][1]), (EXTRA, rows))


def images_kernel(high_ref, low_ref, in_ref, out_ref, given_ref, i_theirs_ref, mine_ref, theirs_ref):
    rows = in_ref.shape[0]
    both = high_ref[...], low_ref[...]
    total = None
    blocks = [halves(in_ref[...]), halves(out_ref[...])]
    coefs = [terms(both, block)[0] for block in blocks]
    for coef, block in zip(coefs, blocks):
        total = weighted(total, coef, block)
    mine_ref[...] = given_ref[...] + total[:rows]
    theirs_ref[:rows, :] = total[rows:]
    theirs_ref[rows:, :] = i_theirs_ref[...]


def far_texts_kernel(
    i_high_ref, i_low_ref, t_high_ref, t_low_ref, block_ref, i_given, l_given, t_given, i_mine_ref, l_mine_ref, t_mine_ref
):
    rows = block_ref.shape[0]
    own, texts, block = (i_high_ref[...], i_low_ref[...]), (t_high_ref[:rows, :], t_low_ref[:rows, :]), halves(block_ref[...])
    coefs, each = terms(own, block, False, True)
    i_mine_ref[...] = weighted(i_given[...], coefs, block)
    l_mine_ref[...] = l_given[...] + as_row(each)
    coefs, _ = terms(texts, own, True)
    t_mine_ref[...] = weighted(t_given[...], coefs, own)


def far_images_kernel(high_ref, low_ref, block_ref, c_high_ref, c_low_ref, b_high_ref, b_low_ref):
    rows = block_ref.shape[0]
    block = halves(block_ref[...])
    b_high_ref[...], b_low_ref[...] = block
    coefs, _ = terms((high_ref[:rows, :], low_ref[:rows, :]), block)
    c_high_ref[...], c_low_ref[...] = halves(coefs)


def last_kernel(
    c_high_ref, c_low_ref, b_high_ref, b_low_ref, i_mine, t_mine, l_mine, theirs, image_ref, text_ref, loss_ref
):
    rows, width = t_mine.shape
    scale = softness_factor / math.sqrt(width)
    image_ref[...] = scale * (i_mine[...] + theirs[rows : 2 * rows, :])
    loss_ref[...] = (l_mine[:1, :] + theirs[2 * rows : 2 * rows + 1, :rows]) * (1.0 / ((2 * CYCLE + 1) * rows))
    high, low, b_high = c_high_ref[...], c_low_ref[...], b_high_ref[...]
    total = dot(high, b_high, 0) + dot(high, b_low_ref[...], 0) + dot(low, b_high, 0)
    text_ref[...] = scale * (total + (t_mine[...] + theirs[:rows, :]))


def call(kernel, outs, *args, flops=1000, **specs):
    return pl.pallas_call(
        kernel,
        out_shape=[jax.ShapeDtypeStruct(shape, dtype) for shape, dtype in outs],
        compiler_params=pltpu.CompilerParams(vmem_limit_bytes=VMEM_LIMIT),
        cost_estimate=pl.CostEstimate(flops=flops, bytes_accessed=1000, transcendentals=0),
        **specs,
    )(*args)


def per_device(images, texts):
    rows, width = images.shape
    f32, bf16 = jnp.float32, jnp.bfloat16
    grad, longer = ((rows, width), f32), ((rows + EXTRA, width), f32)
    most, rest = ((rows - rows // 4, width), f32), ((rows // 4, width), f32)
    low, low2, loss = ((rows, width), bf16), ((2 * rows, width), bf16), ((EXTRA, rows), f32)

    t_in, t_out = inward(texts), outward(texts)
    i_sib = sibling(images)
    *t_parts, i_mine, l_mine, i_high, i_low, t_high, t_low = call(
        own_kernel,
        (most, rest, grad, loss, low, low, low, low),
        images,
        texts,
        in_specs=[pl.BlockSpec(memory_space=pltpu.HBM)] * 2,
        scratch_shapes=[pltpu.VMEM(images.shape, f32)] * 2 + [pltpu.SemaphoreType.DMA((2,))],
    )
    i_in, i_out = inward(after(images, l_mine)), outward(images)
    t_far = across(t_in)
    i_mine, l_mine, t_mine, i_sib_high, i_sib_low = call(
        texts_kernel,
        (grad, loss, grad, low, low),
        i_high, i_low, t_high, t_low, t_in, t_out, i_sib, i_mine, l_mine,
    )
    i_far = across(after(i_in, l_mine))
    t_sib = [sibling(after(part, l_mine)) for part in t_parts]
    i_mine, i_theirs, l_mine, t_high, t_low = call(
        pair_kernel,
        (grad, longer, loss, low2, low2),
        i_sib_high, i_sib_low, *t_sib, t_in, t_out, i_high, i_low, t_high, t_low, i_mine, l_mine,
    )
    t_mine, theirs = call(
        images_kernel, (grad, ((2 * rows + EXTRA, width), f32)), t_high, t_low, i_in, i_out, t_mine, i_theirs
    )
    i_mine, l_mine, t_mine = call(
        far_texts_kernel, (grad, loss, grad), i_high, i_low, t_high, t_low, t_far, i_mine, l_mine, t_mine, flops=FLOPS_C
    )
    theirs = sibling(theirs)
    square = ((rows, rows), bf16)
    found = call(far_images_kernel, (square, square, low, low), t_high, after(t_low, l_mine), i_far, flops=FLOPS_D)
    image_grad, text_grad, pair_loss = call(
        last_kernel, (grad, grad, ((1, rows), f32)), *found, i_mine, t_mine, l_mine, theirs
    )
    return (pair_loss.reshape(rows), image_grad, text_grad)


def solution(mesh):
    return jax.shard_map(
        per_device,
        mesh=mesh,
        in_specs=(P("blk", None), P("blk", None)),
        out_specs=(P("blk"), P("blk", None), P("blk", None)),
        check_vma=False,
    )
```

```python
import functools
import math

import jax
import jax.numpy as jnp
from jax import lax
from jax.experimental import pallas as pl
from jax.experimental.pallas import tpu as pltpu
from jax.sharding import PartitionSpec as P

CYCLE = 3
softness_factor = 2.0
logit_bias = -4.0
EXTRA = 8
FLOPS_C = 2_000_000_000
FLOPS_D = 10_000_000_000
VMEM_LIMIT = 24 * 1024 * 1024


def permuted(value, target):
    count = lax.axis_size("blk")
    return lax.ppermute(value, "blk", [(i, target(i) % count) for i in range(count)])


def sibling(value):
    return permuted(value, lambda i: i ^ 1)


def outward(value):
    return permuted(value, lambda i: i - 2 if i % 2 else i + 2)


def inward(value):
    return permuted(value, lambda i: i + 2 if i % 2 else i - 2)


def across(value):
    return permuted(value, lambda i: i + 1 if i % 2 else i - 1)


def after(value, *others):
    return lax.optimization_barrier((value,) + others)[0]


def halves(x):
    high = x.astype(jnp.bfloat16)
    return high, (x - high.astype(jnp.float32)).astype(jnp.bfloat16)


def dot(a, b, contract_b):
    dims = (((1,), (contract_b,)), ((), ()))
    return lax.dot_general(a, b, dims, preferred_element_type=jnp.float32)


def dots_of(own, block):
    return dot(own[0], block[0], 1) + dot(own[0], block[1], 1) + dot(own[1], block[0], 1)


def weighted(total, coefs, block):
    high, low = halves(coefs)
    first = dot(high, block[0], 0)
    total = first if total is None else total + first
    return total + dot(high, block[1], 0) + dot(low, block[0], 0)


def terms(own, block, positive=False, loss=False):
    scale = softness_factor / math.sqrt(own[0].shape[1])
    x = scale * dots_of(own, block) + logit_bias
    if positive:
        diagonal = lax.broadcasted_iota(jnp.int32, x.shape, 0) == lax.broadcasted_iota(jnp.int32, x.shape, 1)
        x = jnp.where(diagonal, -x, x)
    e = jnp.exp(-jnp.abs(x))
    r = 1.0 / (1.0 + e)
    coefs = jnp.where(x >= 0, r, e * r)
    if positive:
        coefs = jnp.where(diagonal, -coefs, coefs)
    if not loss:
        return coefs, None
    series = e * (1.0 - e * (0.5 - e * (1.0 / 3.0 - e * (0.25 - e * 0.2))))
    each = jnp.maximum(x, 0.0) + jnp.where(e < 0.0625, series, jnp.log(1.0 + e))
    return coefs, each[:, :128] + each[:, 128:]


def as_row(loss):
    return jnp.sum(loss.T, axis=0, keepdims=True)


def own_kernel(
    i_hbm, t_hbm, first_ref, second_ref, i_mine_ref, l_mine_ref, i_high_ref, i_low_ref, t_high_ref, t_low_ref, i_ref, t_ref, sems
):
    copies = [
        pltpu.make_async_copy(source, target, sems.at[k])
        for k, (source, target) in enumerate(((i_hbm, i_ref), (t_hbm, t_ref)))
    ]
    for copy in copies:
        copy.start()
    for copy in copies:
        copy.wait()
    middle = first_ref.shape[0]
    first_ref[...], second_ref[...] = t_ref[:middle, :], t_ref[middle:, :]
    own, texts = halves(i_ref[...]), halves(t_ref[...])
    i_high_ref[...], i_low_ref[...] = own
    t_high_ref[...], t_low_ref[...] = texts
    coefs, lost = terms(own, texts, True, True)
    i_mine_ref[...] = weighted(None, coefs, texts)
    l_mine_ref[...] = jnp.broadcast_to(as_row(lost), l_mine_ref.shape)


def texts_kernel(
    i_high_ref, i_low_ref, t_high_ref, t_low_ref, in_ref, out_ref, i_sib_ref, i_given, l_given,
    i_mine_ref, l_mine_ref, t_mine_ref, high_ref, low_ref,
):
    own, texts, images = (i_high_ref[...], i_low_ref[...]), (t_high_ref[...], t_low_ref[...]), halves(i_sib_ref[...])
    high_ref[...], low_ref[...] = images
    blocks = [halves(in_ref[...]), halves(out_ref[...])]
    found = [terms(own, block, False, True) for block in blocks]
    coefs, _ = terms(texts, images)
    t_mine_ref[...] = weighted(None, coefs, images)
    mine = i_given[...]
    for (coefs, _), block in zip(found, blocks):
        mine = weighted(mine, coefs, block)
    i_mine_ref[...] = mine
    l_mine_ref[...] = l_given[...] + as_row(found[0][1] + found[1][1])


def pair_kernel(
    i_sib_high, i_sib_low, t_sib_first, t_sib_second, in_ref, out_ref, i_high_ref, i_low_ref, t_high_ref, t_low_ref, i_given, l_given,
    i_mine_ref, theirs_ref, l_mine_ref, high_ref, low_ref,
):
    rows = in_ref.shape[0]
    images, texts = (i_sib_high[...], i_sib_low[...]), halves(jnp.concatenate([t_sib_first[...], t_sib_second[...]]))
    high_ref[:rows, :], low_ref[:rows, :] = t_high_ref[...], t_low_ref[...]
    high_ref[rows:, :], low_ref[rows:, :] = texts
    blocks = [halves(in_ref[...]), halves(out_ref[...])]
    coefs, lost = terms((i_high_ref[...], i_low_ref[...]), texts, False, True)
    found = [terms(images, block, False, True) for block in blocks]
    i_mine_ref[...] = weighted(i_given[...], coefs, texts)
    l_mine_ref[...] = l_given[...] + as_row(lost)
    theirs = None
    for (coefs, _), block in zip(found, blocks):
        theirs = weighted(theirs, coefs, block)
    theirs_ref[:rows, :] = theirs
    theirs_ref[rows:, :rows] = jnp.broadcast_to(as_row(found[0][1] + found[1][1]), (EXTRA, rows))


def images_kernel(high_ref, low_ref, in_ref, out_ref, given_ref, i_theirs_ref, mine_ref, theirs_ref):
    rows = in_ref.shape[0]
    both = high_ref[...], low_ref[...]
    total = None
    blocks = [halves(in_ref[...]), halves(out_ref[...])]
    coefs = [terms(both, block)[0] for block in blocks]
    for coef, block in zip(coefs, blocks):
        total = weighted(total, coef, block)
    mine_ref[...] = given_ref[...] + total[:rows]
    theirs_ref[:rows, :] = total[rows:]
    theirs_ref[rows:, :] = i_theirs_ref[...]


def far_texts_kernel(
    i_high_ref, i_low_ref, t_high_ref, t_low_ref, block_ref, i_given, l_given, t_given, i_mine_ref, l_mine_ref, t_mine_ref
):
    rows = block_ref.shape[0]
    own, texts, block = (i_high_ref[...], i_low_ref[...]), (t_high_ref[:rows, :], t_low_ref[:rows, :]), halves(block_ref[...])
    coefs, each = terms(own, block, False, True)
    i_mine_ref[...] = weighted(i_given[...], coefs, block)
    l_mine_ref[...] = l_given[...] + as_row(each)
    coefs, _ = terms(texts, own, True)
    t_mine_ref[...] = weighted(t_given[...], coefs, own)


def far_images_kernel(high_ref, low_ref, block_ref, c_high_ref, c_low_ref, b_high_ref, b_low_ref):
    rows = block_ref.shape[0]
    block = halves(block_ref[...])
    b_high_ref[...], b_low_ref[...] = block
    coefs, _ = terms((high_ref[:rows, :], low_ref[:rows, :]), block)
    c_high_ref[...], c_low_ref[...] = halves(coefs)


def last_kernel(
    c_high_ref, c_low_ref, b_high_ref, b_low_ref, i_mine, t_mine, l_mine, theirs, image_ref, text_ref, loss_ref
):
    rows, width = t_mine.shape
    scale = softness_factor / math.sqrt(width)
    image_ref[...] = scale * (i_mine[...] + theirs[rows : 2 * rows, :])
    loss_ref[...] = (l_mine[:1, :] + theirs[2 * rows : 2 * rows + 1, :rows]) * (1.0 / ((2 * CYCLE + 1) * rows))
    high, low, b_high = c_high_ref[...], c_low_ref[...], b_high_ref[...]
    total = dot(high, b_high, 0) + dot(high, b_low_ref[...], 0) + dot(low, b_high, 0)
    text_ref[...] = scale * (total + (t_mine[...] + theirs[:rows, :]))


def call(kernel, outs, *args, flops=1000, **specs):
    return pl.pallas_call(
        kernel,
        out_shape=[jax.ShapeDtypeStruct(shape, dtype) for shape, dtype in outs],
        compiler_params=pltpu.CompilerParams(vmem_limit_bytes=VMEM_LIMIT),
        cost_estimate=pl.CostEstimate(flops=flops, bytes_accessed=1000, transcendentals=0),
        **specs,
    )(*args)


def per_device(images, texts):
    rows, width = images.shape
    f32, bf16 = jnp.float32, jnp.bfloat16
    grad, longer = ((rows, width), f32), ((rows + EXTRA, width), f32)
    most, rest = ((rows - rows // 4, width), f32), ((rows // 4, width), f32)
    low, low2, loss = ((rows, width), bf16), ((2 * rows, width), bf16), ((EXTRA, rows), f32)

    t_in, t_out = inward(texts), outward(texts)
    *t_parts, i_mine, l_mine, i_high, i_low, t_high, t_low = call(
        own_kernel,
        (most, rest, grad, loss, low, low, low, low),
        images,
        texts,
        in_specs=[pl.BlockSpec(memory_space=pltpu.HBM)] * 2,
        scratch_shapes=[pltpu.VMEM(images.shape, f32)] * 2 + [pltpu.SemaphoreType.DMA((2,))],
    )
    i_sib = sibling(after(images, l_mine))
    i_in, i_out = inward(after(images, l_mine)), outward(images)
    t_far = across(t_in)
    i_mine, l_mine, t_mine, i_sib_high, i_sib_low = call(
        texts_kernel,
        (grad, loss, grad, low, low),
        i_high, i_low, t_high, t_low, t_in, t_out, i_sib, i_mine, l_mine,
    )
    i_far = across(after(i_in, l_mine))
    t_sib = [sibling(after(part, l_mine)) for part in t_parts]
    i_mine, i_theirs, l_mine, t_high, t_low = call(
        pair_kernel,
        (grad, longer, loss, low2, low2),
        i_sib_high, i_sib_low, *t_sib, t_in, t_out, i_high, i_low, t_high, t_low, i_mine, l_mine,
    )
    t_mine, theirs = call(
        images_kernel, (grad, ((2 * rows + EXTRA, width), f32)), t_high, t_low, i_in, i_out, t_mine, i_theirs
    )
    i_mine, l_mine, t_mine = call(
        far_texts_kernel, (grad, loss, grad), i_high, i_low, t_high, t_low, t_far, i_mine, l_mine, t_mine, flops=FLOPS_C
    )
    theirs = sibling(theirs)
    square = ((rows, rows), bf16)
    found = call(far_images_kernel, (square, square, low, low), t_high, after(t_low, l_mine), i_far, flops=FLOPS_D)
    image_grad, text_grad, pair_loss = call(
        last_kernel, (grad, grad, ((1, rows), f32)), *found, i_mine, t_mine, l_mine, theirs
    )
    return (pair_loss.reshape(rows), image_grad, text_grad)


def solution(mesh):
    return jax.shard_map(
        per_device,
        mesh=mesh,
        in_specs=(P("blk", None), P("blk", None)),
        out_specs=(P("blk"), P("blk", None), P("blk", None)),
        check_vma=False,
    )
```

```python
import functools
import math

import jax
import jax.numpy as jnp
from jax import lax
from jax.experimental import pallas as pl
from jax.experimental.pallas import tpu as pltpu
from jax.sharding import PartitionSpec as P

CYCLE = 3
softness_factor = 2.0
logit_bias = -4.0
EXTRA = 8
FLOPS_C = 2_000_000_000
FLOPS_D = 10_000_000_000
VMEM_LIMIT = 24 * 1024 * 1024


def permuted(value, target):
    count = lax.axis_size("blk")
    return lax.ppermute(value, "blk", [(i, target(i) % count) for i in range(count)])


def sibling(value):
    return permuted(value, lambda i: i ^ 1)


def outward(value):
    return permuted(value, lambda i: i - 2 if i % 2 else i + 2)


def inward(value):
    return permuted(value, lambda i: i + 2 if i % 2 else i - 2)


def across(value):
    return permuted(value, lambda i: i + 1 if i % 2 else i - 1)


def after(value, *others):
    return lax.optimization_barrier((value,) + others)[0]


def halves(x):
    high = x.astype(jnp.bfloat16)
    return high, (x - high.astype(jnp.float32)).astype(jnp.bfloat16)


def dot(a, b, contract_b):
    dims = (((1,), (contract_b,)), ((), ()))
    return lax.dot_general(a, b, dims, preferred_element_type=jnp.float32)


def dots_of(own, block):
    return dot(own[0], block[0], 1) + dot(own[0], block[1], 1) + dot(own[1], block[0], 1)


def weighted(total, coefs, block):
    high, low = halves(coefs)
    first = dot(high, block[0], 0)
    total = first if total is None else total + first
    return total + dot(high, block[1], 0) + dot(low, block[0], 0)


def terms(own, block, positive=False, loss=False):
    scale = softness_factor / math.sqrt(own[0].shape[1])
    x = scale * dots_of(own, block) + logit_bias
    if positive:
        diagonal = lax.broadcasted_iota(jnp.int32, x.shape, 0) == lax.broadcasted_iota(jnp.int32, x.shape, 1)
        x = jnp.where(diagonal, -x, x)
    e = jnp.exp(-jnp.abs(x))
    r = 1.0 / (1.0 + e)
    coefs = jnp.where(x >= 0, r, e * r)
    if positive:
        coefs = jnp.where(diagonal, -coefs, coefs)
    if not loss:
        return coefs, None
    series = e * (1.0 - e * (0.5 - e * (1.0 / 3.0 - e * (0.25 - e * 0.2))))
    each = jnp.maximum(x, 0.0) + jnp.where(e < 0.0625, series, jnp.log(1.0 + e))
    return coefs, each[:, :128] + each[:, 128:]


def as_row(loss):
    return jnp.sum(loss.T, axis=0, keepdims=True)


def own_kernel(
    i_hbm, t_hbm, first_ref, second_ref, i_mine_ref, l_mine_ref, i_high_ref, i_low_ref, t_high_ref, t_low_ref, i_ref, t_ref, sems
):
    copies = [
        pltpu.make_async_copy(source, target, sems.at[k])
        for k, (source, target) in enumerate(((i_hbm, i_ref), (t_hbm, t_ref)))
    ]
    for copy in copies:
        copy.start()
    for copy in copies:
        copy.wait()
    middle = first_ref.shape[0]
    first_ref[...], second_ref[...] = t_ref[:middle, :], t_ref[middle:, :]
    own, texts = halves(i_ref[...]), halves(t_ref[...])
    i_high_ref[...], i_low_ref[...] = own
    t_high_ref[...], t_low_ref[...] = texts
    coefs, lost = terms(own, texts, True, True)
    i_mine_ref[...] = weighted(None, coefs, texts)
    l_mine_ref[...] = jnp.broadcast_to(as_row(lost), l_mine_ref.shape)


def texts_kernel(
    i_high_ref, i_low_ref, in_ref, out_ref, i_sib_ref, i_given, l_given,
    i_mine_ref, l_mine_ref, high_ref, low_ref,
):
    own = i_high_ref[...], i_low_ref[...]
    high_ref[...], low_ref[...] = halves(i_sib_ref[...])
    blocks = [halves(in_ref[...]), halves(out_ref[...])]
    found = [terms(own, block, False, True) for block in blocks]
    mine = i_given[...]
    for (coefs, _), block in zip(found, blocks):
        mine = weighted(mine, coefs, block)
    i_mine_ref[...] = mine
    l_mine_ref[...] = l_given[...] + as_row(found[0][1] + found[1][1])


def pair_kernel(
    i_sib_high, i_sib_low, t_sib_first, t_sib_second, in_ref, out_ref, i_high_ref, i_low_ref, t_high_ref, t_low_ref, i_given, l_given,
    i_mine_ref, theirs_ref, l_mine_ref, high_ref, low_ref,
):
    rows = in_ref.shape[0]
    images, texts = (i_sib_high[...], i_sib_low[...]), halves(jnp.concatenate([t_sib_first[...], t_sib_second[...]]))
    high_ref[:rows, :], low_ref[:rows, :] = t_high_ref[...], t_low_ref[...]
    high_ref[rows:, :], low_ref[rows:, :] = texts
    blocks = [halves(in_ref[...]), halves(out_ref[...])]
    coefs, lost = terms((i_high_ref[...], i_low_ref[...]), texts, False, True)
    found = [terms(images, block, False, True) for block in blocks]
    i_mine_ref[...] = weighted(i_given[...], coefs, texts)
    l_mine_ref[...] = l_given[...] + as_row(lost)
    theirs = None
    for (coefs, _), block in zip(found, blocks):
        theirs = weighted(theirs, coefs, block)
    theirs_ref[:rows, :] = theirs
    theirs_ref[rows:, :rows] = jnp.broadcast_to(as_row(found[0][1] + found[1][1]), (EXTRA, rows))


def images_kernel(high_ref, low_ref, in_ref, out_ref, i_theirs_ref, mine_ref, theirs_ref):
    rows = in_ref.shape[0]
    both = high_ref[...], low_ref[...]
    total = None
    blocks = [halves(in_ref[...]), halves(out_ref[...])]
    coefs = [terms(both, block)[0] for block in blocks]
    for coef, block in zip(coefs, blocks):
        total = weighted(total, coef, block)
    mine_ref[...] = total[:rows]
    theirs_ref[:rows, :] = total[rows:]
    theirs_ref[rows:, :] = i_theirs_ref[...]


def far_texts_kernel(
    i_high_ref, i_low_ref, t_high_ref, t_low_ref, sib_high_ref, sib_low_ref, block_ref, i_given, l_given, t_given,
    i_mine_ref, l_mine_ref, t_mine_ref,
):
    rows = block_ref.shape[0]
    own, texts, block = (i_high_ref[...], i_low_ref[...]), (t_high_ref[:rows, :], t_low_ref[:rows, :]), halves(block_ref[...])
    coefs, each = terms(own, block, False, True)
    i_mine_ref[...] = weighted(i_given[...], coefs, block)
    l_mine_ref[...] = l_given[...] + as_row(each)
    coefs, _ = terms(texts, own, True)
    total = weighted(t_given[...], coefs, own)
    images = sib_high_ref[...], sib_low_ref[...]
    coefs, _ = terms(texts, images)
    t_mine_ref[...] = weighted(total, coefs, images)


def far_images_kernel(high_ref, low_ref, block_ref, c_high_ref, c_low_ref, b_high_ref, b_low_ref):
    rows = block_ref.shape[0]
    block = halves(block_ref[...])
    b_high_ref[...], b_low_ref[...] = block
    coefs, _ = terms((high_ref[:rows, :], low_ref[:rows, :]), block)
    c_high_ref[...], c_low_ref[...] = halves(coefs)


def last_kernel(
    c_high_ref, c_low_ref, b_high_ref, b_low_ref, i_mine, t_mine, l_mine, theirs, image_ref, text_ref, loss_ref
):
    rows, width = t_mine.shape
    scale = softness_factor / math.sqrt(width)
    image_ref[...] = scale * (i_mine[...] + theirs[rows : 2 * rows, :])
    loss_ref[...] = (l_mine[:1, :] + theirs[2 * rows : 2 * rows + 1, :rows]) * (1.0 / ((2 * CYCLE + 1) * rows))
    high, low, b_high = c_high_ref[...], c_low_ref[...], b_high_ref[...]
    total = dot(high, b_high, 0) + dot(high, b_low_ref[...], 0) + dot(low, b_high, 0)
    text_ref[...] = scale * (total + (t_mine[...] + theirs[:rows, :]))


def call(kernel, outs, *args, flops=1000, **specs):
    return pl.pallas_call(
        kernel,
        out_shape=[jax.ShapeDtypeStruct(shape, dtype) for shape, dtype in outs],
        compiler_params=pltpu.CompilerParams(vmem_limit_bytes=VMEM_LIMIT),
        cost_estimate=pl.CostEstimate(flops=flops, bytes_accessed=1000, transcendentals=0),
        **specs,
    )(*args)


def per_device(images, texts):
    rows, width = images.shape
    f32, bf16 = jnp.float32, jnp.bfloat16
    grad, longer = ((rows, width), f32), ((rows + EXTRA, width), f32)
    most, rest = ((rows - rows // 4, width), f32), ((rows // 4, width), f32)
    low, low2, loss = ((rows, width), bf16), ((2 * rows, width), bf16), ((EXTRA, rows), f32)

    t_in, t_out = inward(texts), outward(texts)
    i_sib = sibling(images)
    *t_parts, i_mine, l_mine, i_high, i_low, t_high, t_low = call(
        own_kernel,
        (most, rest, grad, loss, low, low, low, low),
        images,
        texts,
        in_specs=[pl.BlockSpec(memory_space=pltpu.HBM)] * 2,
        scratch_shapes=[pltpu.VMEM(images.shape, f32)] * 2 + [pltpu.SemaphoreType.DMA((2,))],
    )
    i_in, i_out = inward(after(images, l_mine)), outward(images)
    t_far = across(t_in)
    i_mine, l_mine, i_sib_high, i_sib_low = call(
        texts_kernel,
        (grad, loss, low, low),
        i_high, i_low, t_in, t_out, i_sib, i_mine, l_mine,
    )
    i_far = across(after(i_in, l_mine))
    t_sib = [sibling(after(part, l_mine)) for part in t_parts]
    i_mine, i_theirs, l_mine, t_high, t_low = call(
        pair_kernel,
        (grad, longer, loss, low2, low2),
        i_sib_high, i_sib_low, *t_sib, t_in, t_out, i_high, i_low, t_high, t_low, i_mine, l_mine,
    )
    t_mine, theirs = call(
        images_kernel, (grad, ((2 * rows + EXTRA, width), f32)), t_high, t_low, i_in, i_out, i_theirs
    )
    i_mine, l_mine, t_mine = call(
        far_texts_kernel, (grad, loss, grad), i_high, i_low, t_high, t_low, i_sib_high, i_sib_low, t_far, i_mine, l_mine, t_mine, flops=FLOPS_C
    )
    theirs = sibling(theirs)
    square = ((rows, rows), bf16)
    found = call(far_images_kernel, (square, square, low, low), t_high, after(t_low, l_mine), i_far, flops=FLOPS_D)
    image_grad, text_grad, pair_loss = call(
        last_kernel, (grad, grad, ((1, rows), f32)), *found, i_mine, t_mine, l_mine, theirs
    )
    return (pair_loss.reshape(rows), image_grad, text_grad)


def solution(mesh):
    return jax.shard_map(
        per_device,
        mesh=mesh,
        in_specs=(P("blk", None), P("blk", None)),
        out_specs=(P("blk"), P("blk", None), P("blk", None)),
        check_vma=False,
    )
```
